32 devices in a mesh: ocx: 4 (over x, core), ocy: 8 (over z, y).
Axes of the slice: x: 2, y: 2, z: 4, core: 2. Of those that a mesh axis runs over, the one named last changes fastest.
Arguments:
- ocean_state: float32 [4, 16, 32, 1024], P(None, None, 'ocx', 'ocy'), may hold values from -6 to 6
- floe_state: float32 [4, 16384], P(None, ('ocx', 'ocy')), may hold values from -6 to 6
- floe_props: float32 [2, 16384], P(None, ('ocx', 'ocy')), may hold values from 0.6 to 1.6
- contact_pairs: int32 [2, 128, 512], P(None, ('ocx', 'ocy')), may hold values from 0 to 127, as said below
- bond_ends: int32 [2, 128, 256], P(None, ('ocx', 'ocy')), may hold values from 0 to 127
- bond_broken: int32 [128, 256], P(('ocx', 'ocy')), may hold values 0 or 1
- couple_floe: int32 [32, 9, 128], P(('ocx', 'ocy')), may hold values from 0 to 511, as said below
- couple_weight: float32 [32, 9, 128], P(('ocx', 'ocy')), may hold values from 0 to 1, as said below
- couple_cell: int32 [32, 9, 128], P(('ocx', 'ocy')), may hold values from 0 to 1023, as said below
Outputs:
- ocean_next: float32 [4, 16, 32, 1024], P(None, None, 'ocx', 'ocy')
- floe_next: float32 [4, 16384], P(None, ('ocx', 'ocy'))
The draws below stay inside these ranges and needn't reach their ends.
Inputs may be any that keep to these rules, and one draw needn't show every extreme that they name: `contact_pairs`: unused slots name one floe twice; live slots name two different floes; a tile has at most 512 live slots and some tiles of every draw have 512. `couple_floe`: every slot, used or not, names a floe of its source device. `couple_weight`: zero exactly on unused slots and positive on used ones; in each bucket the used slots come first; buckets toward blocks outside the ocean are empty; every source device has one bucket with all 128 slots used. `couple_cell`: every slot, used or not, names a surface cell of the ocean block.
All inputs are finite; a program needn't handle non-finite values. No bound on the sum of `bond_broken` on one device may be relied on, other than what follows from the above.
Results may differ from the reference program's by a relative error of at most 0.000065.
Values sent between devices are 32-bit elements; how exact they have to be, the bound alone decides.
A program may use at most 64 MiB of HBM per device.

```python
import math
import jax
import jax.numpy as jnp

CX = 8
CY = 128
LEV = 16
TILE = 128
PAIRS = 512
BONDS = 256
SUBSTEPS = 4
SLOTS = 128
FLOES_DEV = 512
TILES = 128
FLOES = 16384
NX = 32
NY = 1024
N_OCX = 4
N_OCY = 8
DEVICES = 32


def bucket_counts(key):
    sub_key = jax.random.fold_in(key, 4242)
    key_side, key_centre, key_pick = jax.random.split(sub_key, 3)
    device_ids = jnp.arange(DEVICES, dtype=jnp.int32)
    block_row = device_ids // N_OCY
    block_col = device_ids % N_OCY
    near_ids = jnp.arange(9, dtype=jnp.int32)
    target_row = block_row[:, None] + (near_ids // 3 - 1)[None, :]
    target_col = block_col[:, None] + (near_ids % 3 - 1)[None, :]
    inside = (target_row >= 0) & (target_row < N_OCX) & (target_col >= 0) & (target_col < N_OCY)
    side_count = jax.random.randint(key_side, (DEVICES, 9), SLOTS // 8, SLOTS // 2 + 1)
    centre_count = jax.random.randint(key_centre, (DEVICES,), SLOTS // 2, SLOTS + 1)
    counts = side_count.at[:, 4].set(centre_count)
    scores = jax.random.randint(key_pick, (DEVICES, 9), 0, 1000) * 16 + near_ids[None, :]
    scores = jnp.where(inside, scores, -1)
    full_pick = jnp.argmax(scores, axis=1)
    counts = jnp.where(near_ids[None, :] == full_pick[:, None], SLOTS, counts)
    return jnp.where(inside, counts, 0).astype(jnp.int32)


def draw_couple_floe(key, part):
    return jax.random.randint(jax.random.fold_in(key, 101), (DEVICES, 9, SLOTS), 0, FLOES_DEV).astype(jnp.int32)


def draw_couple_cell(key, part):
    return jax.random.randint(jax.random.fold_in(key, 303), (DEVICES, 9, SLOTS), 0, CX * CY).astype(jnp.int32)


def draw_couple_weight(key, part):
    counts = bucket_counts(key)
    slot_index = jnp.arange(SLOTS, dtype=jnp.int32)[None, None, :]
    live_mask = (slot_index < counts[:, :, None]).astype(jnp.float32)
    value_key = jax.random.fold_in(key, 202)
    values = jax.random.uniform(value_key, (DEVICES, 9, SLOTS), jnp.float32, 0.2, 1.0)
    return values * live_mask


def draw_contact_pairs(key, part):
    sub_key = jax.random.fold_in(key, 505)
    key_count, key_hot, key_first, key_step = jax.random.split(sub_key, 4)
    base_count = jax.random.randint(key_count, (TILES,), PAIRS // 6, PAIRS // 2 + 1)
    shuffled = jax.random.permutation(key_hot, TILES)
    hot_mask = jnp.zeros((TILES,), jnp.int32).at[shuffled[:max(1, TILES // 16)]].set(1)
    counts = jnp.where(hot_mask == 1, PAIRS, base_count)
    first_floe = jax.random.randint(key_first, (TILES, PAIRS), 0, TILE)
    stride = jax.random.randint(key_step, (TILES, PAIRS), 1, TILE)
    second = (first_floe + stride) % TILE
    slot_index = jnp.arange(PAIRS, dtype=jnp.int32)[None, :]
    second = jnp.where(slot_index < counts[:, None], second, first_floe)
    return jnp.stack([first_floe, second]).astype(jnp.int32)


def set_ends(array, key, least, high):
    dims = array.shape
    spot = [jax.random.randint(jax.random.fold_in(key, axis), (), 0, dims[axis]) for axis in range(len(dims))]
    array = array.at[tuple(spot)].set(least)
    longest = dims.index(max(dims))
    spot[longest] = (spot[longest] + 1) % dims[longest]
    return array.at[tuple(spot)].set(high)


def block_levels(rng, dims, cuts, smallest, top_value):
    def one(axis_at, parts):
        draws = jax.random.uniform(jax.random.fold_in(jax.random.fold_in(rng, 6), axis_at), (parts,), jnp.float32, smallest / len(cuts), top_value / len(cuts))
        return jnp.repeat(jnp.exp(draws), dims[axis_at] // parts).reshape((-1,) + (1,) * (len(dims) - axis_at - 1))

    level = one(*cuts[0])
    for cut in cuts[1:]:
        level = level * one(*cut)
    return level


def normal_values(stream_key, extent, scale, bound, cuts=(), kind=jnp.bfloat16):
    entries = scale * jax.random.normal(stream_key, extent, jnp.float32)
    if cuts:
        entries = entries * block_levels(stream_key, extent, cuts, -0.22, 0.18)
    return jnp.clip(entries, -bound, bound).astype(kind)


def setup_inputs(seed: int = 0) -> dict:
    splits = jax.random.split(jax.random.key(seed), 10)
    ocean_state = normal_values(splits[0], (4, LEV, NX, NY), 1.0, 6.0, ((2, 4), (3, 8)), jnp.float32)
    floe_state = normal_values(splits[1], (4, FLOES), 1.0, 6.0, ((1, 32),), jnp.float32)
    floe_props = jnp.clip(jnp.exp(math.log(1.6) - 0.98082923 * jax.random.uniform(splits[2], (2, FLOES), jnp.float32) ** block_levels(splits[2], (2, FLOES), ((1, 32),), -0.2, 0.2)), 0.6, 1.6)
    contact_pairs = draw_contact_pairs(jax.random.fold_in(splits[9], 71), 0)
    bond_ends = set_ends(jax.random.randint(splits[4], (2, TILES, BONDS), 0, TILE), jax.random.fold_in(splits[4], 1), 0, TILE - 1).astype(jnp.int32)
    bond_broken = set_ends((jax.random.randint(splits[5], (TILES, BONDS), 0, 4) < 1).astype(jnp.int32), jax.random.fold_in(splits[5], 1), 0, 1)
    couple_floe = draw_couple_floe(jax.random.fold_in(splits[9], 71), 0)
    couple_weight = draw_couple_weight(jax.random.fold_in(splits[9], 71), 0)
    couple_cell = draw_couple_cell(jax.random.fold_in(splits[9], 71), 0)
    return {"ocean_state": ocean_state, "floe_state": floe_state, "floe_props": floe_props, "contact_pairs": contact_pairs, "bond_ends": bond_ends, "bond_broken": bond_broken, "couple_floe": couple_floe, "couple_weight": couple_weight, "couple_cell": couple_cell}


TIME_STEP = 0.05
CONTACT_STIFF = 2.0
CONTACT_DAMP = 0.2
BOND_DAMP = 0.3
DRAG_COEF = 0.5
HEAT_COEF = 0.3
SALT_COEF = 0.2
FREEZE = -1.8
DIFFUSE_SIDE = 0.15
DIFFUSE_DEPTH = 0.2
CORIOLIS = 0.3
PRESSURE_COEF = 0.1
THERMAL_EXP = 0.2
HALINE_CONTR = 0.8


def ocean_update(padded, forcing):
    interior = padded[:, :, 1:-1, 1:-1]
    laplace_side = padded[:, :, 2:, 1:-1] + padded[:, :, :-2, 1:-1] + padded[:, :, 1:-1, 2:] + padded[:, :, 1:-1, :-2] - 4.0 * interior
    above_cells = jnp.concatenate([interior[:, :1], interior[:, :-1]], axis=1)
    below_cells = jnp.concatenate([interior[:, 1:], interior[:, -1:]], axis=1)
    laplace_depth = above_cells + below_cells - 2.0 * interior
    density = HALINE_CONTR * padded[3] - THERMAL_EXP * padded[2]
    pressure = jnp.cumsum(density, axis=0)
    grad_x = 0.5 * (pressure[:, 2:, 1:-1] - pressure[:, :-2, 1:-1])
    grad_y = 0.5 * (pressure[:, 1:-1, 2:] - pressure[:, 1:-1, :-2])
    east_vel = interior[0]
    north_vel = interior[1]
    tendency = DIFFUSE_SIDE * laplace_side + DIFFUSE_DEPTH * laplace_depth
    momentum = jnp.stack([CORIOLIS * north_vel - PRESSURE_COEF * grad_x, -CORIOLIS * east_vel - PRESSURE_COEF * grad_y])
    tendency = tendency.at[:2].add(momentum)
    tendency = tendency.at[:, 0].add(forcing)
    return interior + tendency


def floe_steps(floe_state, floe_props, contact_pairs, bond_ends, bond_broken, intersection_area, drag_sum):
    floe_count = floe_state.shape[1]
    tile_count = floe_count // TILE
    radius = floe_props[0]
    inv_mass = 1.0 / (floe_props[1] * radius * radius)
    offset = (jnp.arange(tile_count, dtype=jnp.int32) * TILE)[:, None]
    first_floe = (contact_pairs[0] + offset).reshape(-1)
    second = (contact_pairs[1] + offset).reshape(-1)
    bond_first = (bond_ends[0] + offset).reshape(-1)
    bond_second = (bond_ends[1] + offset).reshape(-1)
    bond_alive = (1 - bond_broken).astype(jnp.float32).reshape(-1)
    reach_sq = (radius[first_floe] + radius[second]) ** 2
    positions = floe_state[:2]
    velocity = floe_state[2:]
    mean_vel = jnp.zeros_like(velocity)
    for substep in range(SUBSTEPS):
        separation = positions[:, second] - positions[:, first_floe]
        contact_depth = jnp.maximum(1.0 - (separation[0] ** 2 + separation[1] ** 2) / reach_sq, 0.0)
        relative = velocity[:, second] - velocity[:, first_floe]
        pair_force = contact_depth * (CONTACT_DAMP * relative - CONTACT_STIFF * separation)
        bond_force = BOND_DAMP * bond_alive * (velocity[:, bond_second] - velocity[:, bond_first])
        total_force = DRAG_COEF * (drag_sum - intersection_area * velocity)
        total_force = total_force.at[:, first_floe].add(pair_force).at[:, second].add(-pair_force)
        total_force = total_force.at[:, bond_first].add(bond_force).at[:, bond_second].add(-bond_force)
        velocity = velocity + TIME_STEP * inv_mass * total_force
        positions = positions + TIME_STEP * velocity
        mean_vel = mean_vel + velocity / SUBSTEPS
    return jnp.concatenate([positions, velocity], axis=0), mean_vel


def floe_side(floe_state, floe_props, contact_pairs, bond_ends, bond_broken, floe_index, weight, samples):
    floe_count = floe_state.shape[1]
    intersection_area = jnp.zeros((floe_count,), jnp.float32).at[floe_index].add(weight)
    drag_sum = jnp.zeros((2, floe_count), jnp.float32).at[:, floe_index].add(weight * samples[:2])
    floe_next, mean_vel = floe_steps(floe_state, floe_props, contact_pairs, bond_ends, bond_broken, intersection_area, drag_sum)
    ice_vel = mean_vel[:, floe_index]
    stress = DRAG_COEF * weight * (ice_vel - samples[:2])
    heat_flux = HEAT_COEF * weight * (FREEZE - samples[2])
    salt_flux = SALT_COEF * weight * floe_props[1][floe_index]
    return floe_next, jnp.concatenate([stress, heat_flux[None], salt_flux[None]], axis=0)


def reference(ocean_state, floe_state, floe_props, contact_pairs, bond_ends, bond_broken, couple_floe, couple_weight, couple_cell):
    cell_count = CX * CY
    surface = ocean_state[:, 0]
    blocks = surface.reshape(4, N_OCX, CX, N_OCY, CY).transpose(0, 1, 3, 2, 4).reshape(4, DEVICES * cell_count)
    device_ids = jnp.arange(DEVICES, dtype=jnp.int32)
    block_row = device_ids // N_OCY
    block_col = device_ids % N_OCY
    near_ids = jnp.arange(9, dtype=jnp.int32)
    step_x = near_ids // 3 - 1
    step_y = near_ids % 3 - 1
    target_row = block_row[:, None] + step_x[None, :]
    target_col = block_col[:, None] + step_y[None, :]
    inside = (target_row >= 0) & (target_row < N_OCX) & (target_col >= 0) & (target_col < N_OCY)
    target = (jnp.clip(target_row, 0, N_OCX - 1) * N_OCY + jnp.clip(target_col, 0, N_OCY - 1)).astype(jnp.int32)
    back_ids = (8 - near_ids)[None, :]
    cell_at = couple_cell[target, back_ids]
    cell_flat = (target[:, :, None] * cell_count + cell_at).astype(jnp.int32).reshape(-1)
    inside_flat = jnp.broadcast_to(inside[:, :, None], (DEVICES, 9, SLOTS)).astype(jnp.float32).reshape(-1)
    sampled = blocks[:, cell_flat] * inside_flat
    floe_index = (couple_floe + device_ids[:, None, None] * FLOES_DEV).astype(jnp.int32).reshape(-1)
    weight = couple_weight.reshape(-1)
    floe_next, flux = floe_side(floe_state, floe_props, contact_pairs, bond_ends, bond_broken, floe_index, weight, sampled)
    forcing = jnp.zeros((4, DEVICES * cell_count), jnp.float32).at[:, cell_flat].add(flux * inside_flat)
    forcing_grid = forcing.reshape(4, N_OCX, N_OCY, CX, CY).transpose(0, 1, 3, 2, 4).reshape(4, NX, NY)
    padded = jnp.pad(ocean_state, ((0, 0), (0, 0), (1, 1), (1, 1)))
    return ocean_update(padded, forcing_grid), floe_next
```

```python
import functools

import jax
import jax.numpy as jnp
from jax import lax
from jax.experimental import pallas as pl
from jax.experimental.pallas import tpu as pltpu
from jax.sharding import PartitionSpec as P

SUBSTEPS = 4
TIME_STEP = 0.05
CONTACT_STIFF = 2.0
CONTACT_DAMP = 0.2
BOND_DAMP = 0.3
DRAG_COEF = 0.5
HEAT_COEF = 0.3
SALT_COEF = 0.2
FREEZE = -1.8
DIFFUSE_SIDE = 0.15
DIFFUSE_DEPTH = 0.2
CORIOLIS = 0.3
PRESSURE_COEF = 0.1
THERMAL_EXP = 0.2
HALINE_CONTR = 0.8
MESH = pl.DeviceIdType.MESH
F32 = jnp.float32
BF16 = jnp.bfloat16
CENTRE = 4


def lane_gather(field, index):
    return lax.gather(
        field,
        index[..., None],
        lax.GatherDimensionNumbers(
            offset_dims=(),
            collapsed_slice_dims=(1,),
            start_index_map=(1,),
            operand_batching_dims=(0,),
            start_indices_batching_dims=(0,),
        ),
        slice_sizes=(1, 1),
        mode=lax.GatherScatterMode.PROMISE_IN_BOUNDS,
    )


def split(values):
    high = values.astype(BF16).astype(F32)
    return jnp.concatenate([high, values - high], axis=0).astype(BF16)


def product(values, table):
    return lax.dot_general(
        values, table, (((1,), (1,)), ((), ())), preferred_element_type=F32
    )


def hot(mask):
    return jnp.where(mask, 1.0, 0.0).astype(F32)


def kernel(
    mesh_shape,
    ocean,
    floe_state,
    floe_props,
    contact,
    bonds,
    broken,
    c_floe,
    c_weight,
    c_cell,
    ocean_out,
    floe_out,
    msg,
    msg_in,
    flux,
    flux_in,
    row_out,
    row_in,
    col_out,
    col_in,
    pair_table,
    floe_table,
    cell_table,
    state,
    props,
    tend,
    msg_send,
    msg_recv,
    flux_send,
    flux_recv,
    halo_send,
    halo_recv,
):
    size_x, size_y = mesh_shape
    fields, levels, width_x, width_y = ocean.shape
    planes = fields * levels
    buckets, slots = c_cell.shape[1], c_cell.shape[2]
    tiles, pairs = contact.shape[1], contact.shape[2]
    bond_count = bonds.shape[2]
    tile = floe_state.shape[1] // tiles
    rows = 2 * tiles
    at_x, at_y = lax.axis_index("ocx"), lax.axis_index("ocy")

    inside = []
    for n in range(buckets):
        dx, dy = n // 3 - 1, n % 3 - 1
        ok_x = {-1: at_x > 0, 0: at_x >= 0, 1: at_x < size_x - 1}[dx]
        ok_y = {-1: at_y > 0, 0: at_y >= 0, 1: at_y < size_y - 1}[dy]
        inside.append(jnp.logical_and(ok_x, ok_y))
    others = [n for n in range(buckets) if n != CENTRE]
    sides = [1, 7, 3, 5]

    def place(n):
        return (at_x + (n // 3 - 1), at_y + (n % 3 - 1))

    barrier = pltpu.get_barrier_semaphore()
    for n in others:

        @pl.when(inside[n])
        def _(n=n):
            pl.semaphore_signal(barrier, inc=1, device_id=place(n), device_id_type=MESH)

    def copy(src, dst, send, recv, n):
        return pltpu.make_async_remote_copy(
            src_ref=src,
            dst_ref=dst,
            send_sem=send,
            recv_sem=recv,
            device_id=place(n),
            device_id_type=MESH,
        )

    def msg_copy(n):
        return copy(msg.at[n], msg_in.at[8 - n], msg_send.at[n], msg_recv.at[8 - n], n)

    def flux_copy(n):
        return copy(flux.at[n], flux_in.at[8 - n], flux_send.at[n], flux_recv.at[8 - n], n)

    def halo_copy(side):
        pair = side // 2
        src, dst = (row_out, row_in) if pair == 0 else (col_out, col_in)
        mine, there = side % 2, 1 - side % 2
        return copy(
            src.at[mine],
            dst.at[there],
            halo_send.at[side],
            halo_recv.at[2 * pair + there],
            sides[side],
        )

    def msg_arrival(n):
        return copy(msg.at[8 - n], msg_in.at[n], msg_send.at[8 - n], msg_recv.at[n], n)

    def flux_arrival(n):
        return copy(flux.at[8 - n], flux_in.at[n], flux_send.at[8 - n], flux_recv.at[n], n)

    def halo_arrival(side):
        pair = side // 2
        src, dst = (row_out, row_in) if pair == 0 else (col_out, col_in)
        return copy(
            src.at[1 - side % 2],
            dst.at[side % 2],
            halo_send.at[side],
            halo_recv.at[side],
            sides[side],
        )

    row8 = lax.broadcasted_iota(jnp.int32, (8, width_y), 0)
    lane8 = lax.broadcasted_iota(jnp.int32, (8, width_y), 1)
    low = row8 < tiles
    row_tile = jnp.where(low, row8, row8 - tiles)

    def wide(ref_row):
        return jnp.broadcast_to(ref_row, (8, slots))

    for t in range(tiles):
        lanes = pl.ds(t * tile, tile)
        for c in range(2):
            state[0, pl.ds(c * tiles + t, 1), :] = floe_state[pl.ds(c, 1), lanes]
            state[1, pl.ds(c * tiles + t, 1), :] = floe_state[pl.ds(2 + c, 1), lanes]
            props[0, pl.ds(c * tiles + t, 1), :] = floe_props[pl.ds(0, 1), lanes]
            props[1, pl.ds(c * tiles + t, 1), :] = floe_props[pl.ds(1, 1), lanes]
    east, north = ocean[0, 0], ocean[1, 0]
    thick = props[1]
    floe_lane, floe_mask = [], []
    for n in range(buckets):
        cell = wide(c_cell[0, pl.ds(n, 1), :])
        cell_row, cell_lane = cell // width_y, cell % width_y
        floe = wide(c_floe[0, pl.ds(n, 1), :])
        floe_lane.append(floe % tile)
        floe_mask.append(floe // tile == row_tile)
        weight = wide(c_weight[0, pl.ds(n, 1), :])
        here = cell_row == row8
        first = jnp.where(here, lane_gather(east, cell_lane), 0.0)
        second = jnp.where(here, lane_gather(north, cell_lane), 0.0)
        first = first + pltpu.roll(first, 4, 0)
        second = second + pltpu.roll(second, 4, 0)
        both = jnp.where(low, first, second)
        both = both + pltpu.roll(both, 7, 0)
        both = both + pltpu.roll(both, 6, 0)
        msg[n] = both
        other = jnp.where(floe_mask[n], lane_gather(thick, floe_lane[n]), 0.0)
        other = other + pltpu.roll(other, 7, 0)
        other = other + pltpu.roll(other, 6, 0)
        msg[n, pl.ds(1, 1), :] = weight[0:1]
        msg[n, pl.ds(2, 1), :] = weight[0:1] * other[0:1]

    pl.semaphore_wait(barrier, sum(inside[n].astype(jnp.int32) for n in others))
    for n in others:

        @pl.when(inside[n])
        def _(n=n):
            msg_copy(n).start()

    msg_in[CENTRE] = msg[CENTRE]

    flat = ocean.reshape(planes * width_x, width_y)
    row_out[0] = flat[pl.ds(0, planes, stride=width_x), :]
    row_out[1] = flat[pl.ds(width_x - 1, planes, stride=width_x), :]
    lanes_f = lax.broadcasted_iota(jnp.int32, (fields, 8, width_y), 2)
    west = jnp.zeros((fields, 8, width_y), F32)
    side_e = jnp.zeros((fields, 8, width_y), F32)
    for k in range(levels):
        level = ocean[:, k]
        west = jnp.where(lanes_f == k, pltpu.roll(level, k, 2) if k else level, west)
        side_e = jnp.where(lanes_f == k, pltpu.roll(level, k + 1, 2), side_e)
    col_out[0] = west
    col_out[1] = side_e
    for side in range(4):

        @pl.when(inside[sides[side]])
        def _(side=side):
            halo_copy(side).start()

    low_row = lax.broadcasted_iota(jnp.int32, (tile, slots), 0)
    for n in range(buckets):
        floe = c_floe[0, pl.ds(n, 1), :] % tile
        cell = c_cell[0, pl.ds(n, 1), :] % width_y
        lanes = pl.ds(n * slots, slots)
        floe_table[:, lanes] = hot(low_row == floe).astype(BF16)
        cell_table[:, lanes] = hot(low_row == cell).astype(BF16)
    span = 128
    contact_chunks, bond_chunks = pairs // span, bond_count // span
    wide_row = lax.broadcasted_iota(jnp.int32, (tile, span), 0)
    for t in range(tiles):
        for c in range(contact_chunks + bond_chunks):
            ref, at = (contact, c) if c < contact_chunks else (bonds, c - contact_chunks)
            lanes = pl.ds(at * span, span)
            head = ref[0, pl.ds(t, 1), lanes]
            tail = ref[1, pl.ds(t, 1), lanes]
            pair_table[pl.ds(t * tile, tile), pl.ds(c * span, span)] = (
                hot(wide_row == head) - hot(wide_row == tail)
            ).astype(BF16)

    def twice(array):
        return jnp.concatenate([array, array], axis=0)

    positions, velocity = state[0], state[1]
    radius = props[0]
    inv_mass = TIME_STEP / (thick * radius * radius)
    ends, inv_reach = [], []
    for c in range(contact_chunks):
        lanes = pl.ds(c * span, span)
        head, tail = twice(contact[0, :, lanes]), twice(contact[1, :, lanes])
        reach = lane_gather(radius, head) + lane_gather(radius, tail)
        ends.append((head, tail))
        inv_reach.append(1.0 / (reach * reach))
    bond_ends, bond_coef = [], []
    for c in range(bond_chunks):
        lanes = pl.ds(c * span, span)
        bond_ends.append((twice(bonds[0, :, lanes]), twice(bonds[1, :, lanes])))
        bond_coef.append(BOND_DAMP * (1 - twice(broken[:, lanes])).astype(F32))

    def contact_force(positions, velocity):
        forces = []
        for (head, tail), inv in zip(ends, inv_reach):
            separation = lane_gather(positions, tail) - lane_gather(positions, head)
            relative = lane_gather(velocity, tail) - lane_gather(velocity, head)
            square = separation * separation
            square = square + pltpu.roll(square, tiles, 0)
            depth = jnp.maximum(1.0 - square * inv, 0.0)
            forces.append(depth * (CONTACT_DAMP * relative - CONTACT_STIFF * separation))
        for (head, tail), coef in zip(bond_ends, bond_coef):
            forces.append(coef * (lane_gather(velocity, tail) - lane_gather(velocity, head)))
        spread = product(split(jnp.concatenate(forces, axis=1)), pair_table[...])
        spread = spread[:rows] + spread[rows:]
        total = jnp.zeros((rows, tile), F32)
        for t in range(tiles):
            total = jnp.where(row_tile == t, spread[:, t * tile : (t + 1) * tile], total)
        return total

    force = contact_force(positions, velocity)

    def per_floe(values):
        total = product(split(jnp.concatenate(values, axis=1)), floe_table[...])
        return total[:rows] + total[rows:]

    weights = [wide(c_weight[0, pl.ds(n, 1), :]) for n in range(buckets)]
    masked = [jnp.where(m, w, 0.0) for m, w in zip(floe_mask, weights)]
    area = DRAG_COEF * per_floe(masked)

    for n in others:

        @pl.when(inside[n])
        def _(n=n):
            msg_arrival(n).wait_recv()

        @pl.when(jnp.logical_not(inside[n]))
        def _(n=n):
            msg_in[n] = jnp.zeros((8, slots), F32)

    samples = [
        jnp.where(low, wide(msg_in[n, pl.ds(0, 1), :]), wide(msg_in[n, pl.ds(4, 1), :]))
        for n in range(buckets)
    ]
    drag = DRAG_COEF * per_floe([m * s for m, s in zip(masked, samples)])

    mean_vel = jnp.zeros_like(velocity)
    for substep in range(SUBSTEPS):
        if substep:
            force = contact_force(positions, velocity)
        velocity = velocity + inv_mass * (drag - area * velocity + force)
        positions = positions + TIME_STEP * velocity
        mean_vel = mean_vel + velocity / SUBSTEPS

    for n in range(buckets):
        speed = jnp.where(floe_mask[n], lane_gather(mean_vel, floe_lane[n]), 0.0)
        speed = speed + pltpu.roll(speed, 7, 0)
        speed = speed + pltpu.roll(speed, 6, 0)
        flux[n] = weights[n] * speed
    for n in others:

        @pl.when(inside[n])
        def _(n=n):
            flux_copy(n).start()

    flux_in[CENTRE] = flux[CENTRE]
    state[0] = positions
    state[1] = velocity
    for t in range(tiles):
        lanes = pl.ds(t * tile, tile)
        for c in range(2):
            floe_out[pl.ds(c, 1), lanes] = state[0, pl.ds(c * tiles + t, 1), :]
            floe_out[pl.ds(2 + c, 1), lanes] = state[1, pl.ds(c * tiles + t, 1), :]

    here = [
        c_cell[0, pl.ds(n, 1), :] // width_y == row8 for n in range(buckets)
    ]

    def per_cell(ref, first, second):
        values = [
            jnp.concatenate(
                [
                    jnp.where(here[n], wide(ref[n, pl.ds(first, 1), :]), 0.0),
                    jnp.where(here[n], wide(ref[n, pl.ds(second, 1), :]), 0.0),
                ],
                axis=0,
            )
            for n in range(buckets)
        ]
        total = product(split(jnp.concatenate(values, axis=1)), cell_table[...])
        total = total[:16] + total[16:]
        return total[:8], total[8:]

    cover, salt = per_cell(msg_in, 1, 2)

    for side in range(4):

        @pl.when(inside[sides[side]])
        def _(side=side):
            halo_arrival(side).wait_recv()

        @pl.when(jnp.logical_not(inside[sides[side]]))
        def _(side=side):
            dst = row_in if side < 2 else col_in
            dst[side % 2] = jnp.zeros(dst.shape[1:], F32)

    rows_f = lax.broadcasted_iota(jnp.int32, (fields, 8, width_y), 1)
    top, bottom = rows_f == 0, rows_f == width_x - 1
    leftmost, rightmost = lanes_f == 0, lanes_f == width_y - 1
    sum_x = jnp.zeros((8, width_y), F32)
    sum_y = jnp.zeros((8, width_y), F32)
    for k in range(levels):
        level = ocean[:, k]
        before = jnp.stack([row_in[0, pl.ds(f * levels + k, 1), :] for f in range(fields)])
        after = jnp.stack([row_in[1, pl.ds(f * levels + k, 1), :] for f in range(fields)])
        up = jnp.where(top, before, pltpu.roll(level, 1, 1))
        down = jnp.where(bottom, after, pltpu.roll(level, width_x - 1, 1))
        left_in = pltpu.roll(col_in[0], width_y - k, 2) if k else col_in[0]
        right_in = pltpu.roll(col_in[1], width_y - 1 - k, 2)
        left = jnp.where(leftmost, left_in, pltpu.roll(level, 1, 2))
        right = jnp.where(rightmost, right_in, pltpu.roll(level, width_y - 1, 2))
        above = ocean[:, max(k - 1, 0)]
        below = ocean[:, min(k + 1, levels - 1)]
        centre = 1.0 - 4.0 * DIFFUSE_SIDE - 2.0 * DIFFUSE_DEPTH
        new = (
            centre * level
            + DIFFUSE_SIDE * (up + down + left + right)
            + DIFFUSE_DEPTH * (above + below)
        )
        slope_x, slope_y = down - up, right - left
        sum_x = sum_x + (HALINE_CONTR * slope_x[3] - THERMAL_EXP * slope_x[2])
        sum_y = sum_y + (HALINE_CONTR * slope_y[3] - THERMAL_EXP * slope_y[2])
        ocean_out[0, k] = new[0] + CORIOLIS * level[1] - (0.5 * PRESSURE_COEF) * sum_x
        ocean_out[1, k] = new[1] - CORIOLIS * level[0] - (0.5 * PRESSURE_COEF) * sum_y
        if k == 0:
            ocean_out[2, k] = new[2] + HEAT_COEF * (FREEZE - level[2]) * cover
            ocean_out[3, k] = new[3] + SALT_COEF * salt
        else:
            ocean_out[2, k] = new[2]
            ocean_out[3, k] = new[3]

    for n in others:

        @pl.when(inside[n])
        def _(n=n):
            flux_arrival(n).wait_recv()

        @pl.when(jnp.logical_not(inside[n]))
        def _(n=n):
            flux_in[n] = jnp.zeros((8, slots), F32)

    push_x, push_y = per_cell(flux_in, 0, 4)
    ocean_out[0, 0] += DRAG_COEF * (push_x - ocean[0, 0] * cover)
    ocean_out[1, 0] += DRAG_COEF * (push_y - ocean[1, 0] * cover)

    for n in others:

        @pl.when(inside[n])
        def _(n=n):
            msg_copy(n).wait_send()
            flux_copy(n).wait_send()

    for side in range(4):

        @pl.when(inside[sides[side]])
        def _(side=side):
            halo_copy(side).wait_send()


def shards(mesh_shape, *args):
    ocean_state, floe_state, _, contact_pairs, bond_ends = args[:5]
    couple_cell = args[8]
    fields, levels, width_x, width_y = ocean_state.shape
    tiles, pairs = contact_pairs.shape[1:]
    bond_count = bond_ends.shape[2]
    floes = floe_state.shape[1]
    tile = floes // tiles
    buckets, slots = couple_cell.shape[1:]
    assert width_x == 8 and 2 * tiles == 8 and tile == slots == width_y == 128
    vmem = pl.BlockSpec(memory_space=pltpu.VMEM)
    dma = pltpu.SemaphoreType.DMA
    return pl.pallas_call(
        functools.partial(kernel, mesh_shape),
        out_shape=(
            jax.ShapeDtypeStruct(ocean_state.shape, F32),
            jax.ShapeDtypeStruct(floe_state.shape, F32),
        ),
        in_specs=[vmem] * 9,
        out_specs=(vmem, vmem),
        scratch_shapes=[
            pltpu.VMEM((buckets, 8, slots), F32),
            pltpu.VMEM((buckets, 8, slots), F32),
            pltpu.VMEM((buckets, 8, slots), F32),
            pltpu.VMEM((buckets, 8, slots), F32),
            pltpu.VMEM((2, fields * levels, width_y), F32),
            pltpu.VMEM((2, fields * levels, width_y), F32),
            pltpu.VMEM((2, fields, width_x, width_y), F32),
            pltpu.VMEM((2, fields, width_x, width_y), F32),
            pltpu.VMEM((floes, pairs + bond_count), BF16),
            pltpu.VMEM((tile, buckets * slots), BF16),
            pltpu.VMEM((width_y, buckets * slots), BF16),
            pltpu.VMEM((2, 2 * tiles, tile), F32),
            pltpu.VMEM((2, 2 * tiles, tile), F32),
            pltpu.VMEM((2, width_x, width_y), F32),
            dma((buckets,)),
            dma((buckets,)),
            dma((buckets,)),
            dma((buckets,)),
            dma((4,)),
            dma((4,)),
        ],
        compiler_params=pltpu.CompilerParams(
            collective_id=0, has_side_effects=True, vmem_limit_bytes=24 * 1024 * 1024
        ),
        cost_estimate=pl.CostEstimate(
            flops=200_000_000, bytes_accessed=1_000_000, transcendentals=0
        ),
    )(*args)


def solution(mesh):
    in_specs = (
        P(None, None, "ocx", "ocy"),
        P(None, ("ocx", "ocy")),
        P(None, ("ocx", "ocy")),
        P(None, ("ocx", "ocy"), None),
        P(None, ("ocx", "ocy"), None),
        P(("ocx", "ocy"), None),
        P(("ocx", "ocy"), None, None),
        P(("ocx", "ocy"), None, None),
        P(("ocx", "ocy"), None, None),
    )
    out_specs = (P(None, None, "ocx", "ocy"), P(None, ("ocx", "ocy")))
    body = functools.partial(shards, (mesh.shape["ocx"], mesh.shape["ocy"]))
    return jax.shard_map(body, mesh=mesh, in_specs=in_specs, out_specs=out_specs, check_vma=False)
```

```python
import functools

import jax
import jax.numpy as jnp
from jax import lax
from jax.experimental import pallas as pl
from jax.experimental.pallas import tpu as pltpu
from jax.sharding import PartitionSpec as P

SUBSTEPS = 4
TIME_STEP = 0.05
CONTACT_STIFF = 2.0
CONTACT_DAMP = 0.2
BOND_DAMP = 0.3
DRAG_COEF = 0.5
HEAT_COEF = 0.3
SALT_COEF = 0.2
FREEZE = -1.8
DIFFUSE_SIDE = 0.15
DIFFUSE_DEPTH = 0.2
CORIOLIS = 0.3
PRESSURE_COEF = 0.1
THERMAL_EXP = 0.2
HALINE_CONTR = 0.8
MESH = pl.DeviceIdType.MESH
F32 = jnp.float32
BF16 = jnp.bfloat16
CENTRE = 4


def lane_gather(field, index):
    return lax.gather(
        field,
        index[..., None],
        lax.GatherDimensionNumbers(
            offset_dims=(),
            collapsed_slice_dims=(1,),
            start_index_map=(1,),
            operand_batching_dims=(0,),
            start_indices_batching_dims=(0,),
        ),
        slice_sizes=(1, 1),
        mode=lax.GatherScatterMode.PROMISE_IN_BOUNDS,
    )


def split(values):
    high = values.astype(BF16).astype(F32)
    return jnp.concatenate([high, values - high], axis=0).astype(BF16)


def product(values, table):
    return lax.dot_general(
        values, table, (((1,), (1,)), ((), ())), preferred_element_type=F32
    )


def hot(mask):
    return jnp.where(mask, 1.0, 0.0).astype(F32)


def kernel(
    mesh_shape,
    ocean_hbm,
    floe_state_hbm,
    floe_props_hbm,
    contact_hbm,
    bonds_hbm,
    broken_hbm,
    c_floe_hbm,
    c_weight_hbm,
    c_cell_hbm,
    ocean_out,
    floe_out,
    msg,
    msg_in,
    flux,
    flux_in,
    row_out,
    row_in,
    col_out,
    col_in,
    pair_table,
    floe_table,
    cell_table,
    state,
    props,
    ocean,
    surface,
    floe_state,
    floe_props,
    contact,
    bonds,
    broken,
    c_floe,
    c_weight,
    c_cell,
    load_sem,
    msg_send,
    msg_recv,
    flux_send,
    flux_recv,
    halo_send,
    halo_recv,
):
    size_x, size_y = mesh_shape
    fields, levels, width_x, width_y = ocean.shape
    planes = fields * levels
    buckets, slots = c_cell.shape[0], c_cell.shape[2]
    tiles, pairs = contact.shape[1], contact.shape[2]
    bond_count = bonds.shape[2]
    tile = floe_state.shape[1] // tiles
    rows = 2 * tiles
    at_x, at_y = lax.axis_index("ocx"), lax.axis_index("ocy")

    inside = []
    for n in range(buckets):
        dx, dy = n // 3 - 1, n % 3 - 1
        ok_x = {-1: at_x > 0, 0: at_x >= 0, 1: at_x < size_x - 1}[dx]
        ok_y = {-1: at_y > 0, 0: at_y >= 0, 1: at_y < size_y - 1}[dy]
        inside.append(jnp.logical_and(ok_x, ok_y))
    others = [n for n in range(buckets) if n != CENTRE]
    sides = [1, 7, 3, 5]

    def place(n):
        return (at_x + (n // 3 - 1), at_y + (n % 3 - 1))

    barrier = pltpu.get_barrier_semaphore()
    for n in others:

        @pl.when(inside[n])
        def _(n=n):
            pl.semaphore_signal(barrier, inc=1, device_id=place(n), device_id_type=MESH)

    loads = [
        pltpu.make_async_copy(src, dst, load_sem.at[at])
        for at, (src, dst) in enumerate(
            [
                (c_cell_hbm, c_cell),
                (ocean_hbm.at[pl.ds(0, 2), 0], surface),
                (c_floe_hbm, c_floe),
                (floe_props_hbm, floe_props),
                (c_weight_hbm, c_weight),
                (floe_state_hbm, floe_state),
                (ocean_hbm, ocean),
                (contact_hbm, contact),
                (bonds_hbm, bonds),
                (broken_hbm, broken),
            ]
        )
    ]
    for load in loads:
        load.start()

    def copy(src, dst, send, recv, n):
        return pltpu.make_async_remote_copy(
            src_ref=src,
            dst_ref=dst,
            send_sem=send,
            recv_sem=recv,
            device_id=place(n),
            device_id_type=MESH,
        )

    def msg_copy(n):
        return copy(msg.at[n], msg_in.at[8 - n], msg_send.at[n], msg_recv.at[8 - n], n)

    def flux_copy(n):
        return copy(flux.at[n], flux_in.at[8 - n], flux_send.at[n], flux_recv.at[8 - n], n)

    def halo_copy(side):
        pair = side // 2
        src, dst = (row_out, row_in) if pair == 0 else (col_out, col_in)
        mine, there = side % 2, 1 - side % 2
        return copy(
            src.at[mine],
            dst.at[there],
            halo_send.at[side],
            halo_recv.at[2 * pair + there],
            sides[side],
        )

    def msg_arrival(n):
        return copy(msg.at[8 - n], msg_in.at[n], msg_send.at[8 - n], msg_recv.at[n], n)

    def flux_arrival(n):
        return copy(flux.at[8 - n], flux_in.at[n], flux_send.at[8 - n], flux_recv.at[n], n)

    def halo_arrival(side):
        pair = side // 2
        src, dst = (row_out, row_in) if pair == 0 else (col_out, col_in)
        return copy(
            src.at[1 - side % 2],
            dst.at[side % 2],
            halo_send.at[side],
            halo_recv.at[side],
            sides[side],
        )

    row8 = lax.broadcasted_iota(jnp.int32, (8, width_y), 0)
    lane8 = lax.broadcasted_iota(jnp.int32, (8, width_y), 1)
    low = row8 < tiles
    row_tile = jnp.where(low, row8, row8 - tiles)

    def wide(ref_row):
        return jnp.broadcast_to(ref_row, (8, slots))

    for load in loads[:6]:
        load.wait()

    for t in range(tiles):
        lanes = pl.ds(t * tile, tile)
        for c in range(2):
            state[0, pl.ds(c * tiles + t, 1), :] = floe_state[pl.ds(c, 1), lanes]
            state[1, pl.ds(c * tiles + t, 1), :] = floe_state[pl.ds(2 + c, 1), lanes]
            props[0, pl.ds(c * tiles + t, 1), :] = floe_props[pl.ds(0, 1), lanes]
            props[1, pl.ds(c * tiles + t, 1), :] = floe_props[pl.ds(1, 1), lanes]
    east, north = surface[0], surface[1]
    thick = props[1]
    floe_lane, floe_mask = [], []
    for n in range(buckets):
        cell = wide(c_cell[n])
        cell_row, cell_lane = cell // width_y, cell % width_y
        floe = wide(c_floe[n])
        floe_lane.append(floe % tile)
        floe_mask.append(floe // tile == row_tile)
        weight = wide(c_weight[n])
        here = cell_row == row8
        first = jnp.where(here, lane_gather(east, cell_lane), 0.0)
        second = jnp.where(here, lane_gather(north, cell_lane), 0.0)
        first = first + pltpu.roll(first, 4, 0)
        second = second + pltpu.roll(second, 4, 0)
        both = jnp.where(low, first, second)
        both = both + pltpu.roll(both, 7, 0)
        both = both + pltpu.roll(both, 6, 0)
        msg[n] = both
        other = jnp.where(floe_mask[n], lane_gather(thick, floe_lane[n]), 0.0)
        other = other + pltpu.roll(other, 7, 0)
        other = other + pltpu.roll(other, 6, 0)
        msg[n, pl.ds(1, 1), :] = weight[0:1]
        msg[n, pl.ds(2, 1), :] = weight[0:1] * other[0:1]

    pl.semaphore_wait(barrier, sum(inside[n].astype(jnp.int32) for n in others))
    for n in others:

        @pl.when(inside[n])
        def _(n=n):
            msg_copy(n).start()

    msg_in[CENTRE] = msg[CENTRE]
    for load in loads[6:]:
        load.wait()

    flat = ocean.reshape(planes * width_x, width_y)
    row_out[0] = flat[pl.ds(0, planes, stride=width_x), :]
    row_out[1] = flat[pl.ds(width_x - 1, planes, stride=width_x), :]
    lanes_f = lax.broadcasted_iota(jnp.int32, (fields, 8, width_y), 2)
    west = jnp.zeros((fields, 8, width_y), F32)
    side_e = jnp.zeros((fields, 8, width_y), F32)
    for k in range(levels):
        level = ocean[:, k]
        west = jnp.where(lanes_f == k, pltpu.roll(level, k, 2) if k else level, west)
        side_e = jnp.where(lanes_f == k, pltpu.roll(level, k + 1, 2), side_e)
    col_out[0] = west
    col_out[1] = side_e
    for side in range(4):

        @pl.when(inside[sides[side]])
        def _(side=side):
            halo_copy(side).start()

    low_row = lax.broadcasted_iota(jnp.int32, (tile, slots), 0)
    for n in range(buckets):
        floe = c_floe[n] % tile
        cell = c_cell[n] % width_y
        lanes = pl.ds(n * slots, slots)
        floe_table[:, lanes] = hot(low_row == floe).astype(BF16)
        cell_table[:, lanes] = hot(low_row == cell).astype(BF16)
    span = 128
    contact_chunks, bond_chunks = pairs // span, bond_count // span
    wide_row = lax.broadcasted_iota(jnp.int32, (tile, span), 0)
    for t in range(tiles):
        for c in range(contact_chunks + bond_chunks):
            ref, at = (contact, c) if c < contact_chunks else (bonds, c - contact_chunks)
            lanes = pl.ds(at * span, span)
            head = ref[0, pl.ds(t, 1), lanes]
            tail = ref[1, pl.ds(t, 1), lanes]
            pair_table[pl.ds(t * tile, tile), pl.ds(c * span, span)] = (
                hot(wide_row == head) - hot(wide_row == tail)
            ).astype(BF16)

    def twice(array):
        return jnp.concatenate([array, array], axis=0)

    positions, velocity = state[0], state[1]
    radius = props[0]
    inv_mass = TIME_STEP / (thick * radius * radius)
    ends, inv_reach = [], []
    for c in range(contact_chunks):
        lanes = pl.ds(c * span, span)
        head, tail = twice(contact[0, :, lanes]), twice(contact[1, :, lanes])
        reach = lane_gather(radius, head) + lane_gather(radius, tail)
        ends.append((head, tail))
        inv_reach.append(1.0 / (reach * reach))
    bond_ends, bond_coef = [], []
    for c in range(bond_chunks):
        lanes = pl.ds(c * span, span)
        bond_ends.append((twice(bonds[0, :, lanes]), twice(bonds[1, :, lanes])))
        bond_coef.append(BOND_DAMP * (1 - twice(broken[:, lanes])).astype(F32))

    def contact_force(positions, velocity):
        forces = []
        for (head, tail), inv in zip(ends, inv_reach):
            separation = lane_gather(positions, tail) - lane_gather(positions, head)
            relative = lane_gather(velocity, tail) - lane_gather(velocity, head)
            square = separation * separation
            square = square + pltpu.roll(square, tiles, 0)
            depth = jnp.maximum(1.0 - square * inv, 0.0)
            forces.append(depth * (CONTACT_DAMP * relative - CONTACT_STIFF * separation))
        for (head, tail), coef in zip(bond_ends, bond_coef):
            forces.append(coef * (lane_gather(velocity, tail) - lane_gather(velocity, head)))
        spread = product(split(jnp.concatenate(forces, axis=1)), pair_table[...])
        spread = spread[:rows] + spread[rows:]
        total = jnp.zeros((rows, tile), F32)
        for t in range(tiles):
            total = jnp.where(row_tile == t, spread[:, t * tile : (t + 1) * tile], total)
        return total

    force = contact_force(positions, velocity)

    def per_floe(values):
        total = product(split(jnp.concatenate(values, axis=1)), floe_table[...])
        return total[:rows] + total[rows:]

    weights = [wide(c_weight[n]) for n in range(buckets)]
    masked = [jnp.where(m, w, 0.0) for m, w in zip(floe_mask, weights)]
    area = DRAG_COEF * per_floe(masked)

    for n in others:

        @pl.when(inside[n])
        def _(n=n):
            msg_arrival(n).wait_recv()

        @pl.when(jnp.logical_not(inside[n]))
        def _(n=n):
            msg_in[n] = jnp.zeros((8, slots), F32)

    samples = [
        jnp.where(low, wide(msg_in[n, pl.ds(0, 1), :]), wide(msg_in[n, pl.ds(4, 1), :]))
        for n in range(buckets)
    ]
    drag = DRAG_COEF * per_floe([m * s for m, s in zip(masked, samples)])

    mean_vel = jnp.zeros_like(velocity)
    for substep in range(SUBSTEPS):
        if substep:
            force = contact_force(positions, velocity)
        velocity = velocity + inv_mass * (drag - area * velocity + force)
        positions = positions + TIME_STEP * velocity
        mean_vel = mean_vel + velocity / SUBSTEPS

    for n in range(buckets):
        speed = jnp.where(floe_mask[n], lane_gather(mean_vel, floe_lane[n]), 0.0)
        speed = speed + pltpu.roll(speed, 7, 0)
        speed = speed + pltpu.roll(speed, 6, 0)
        flux[n] = weights[n] * speed
    for n in others:

        @pl.when(inside[n])
        def _(n=n):
            flux_copy(n).start()

    flux_in[CENTRE] = flux[CENTRE]
    state[0] = positions
    state[1] = velocity
    for t in range(tiles):
        lanes = pl.ds(t * tile, tile)
        for c in range(2):
            floe_out[pl.ds(c, 1), lanes] = state[0, pl.ds(c * tiles + t, 1), :]
            floe_out[pl.ds(2 + c, 1), lanes] = state[1, pl.ds(c * tiles + t, 1), :]

    here = [
        c_cell[n] // width_y == row8 for n in range(buckets)
    ]

    def per_cell(ref, first, second):
        values = [
            jnp.concatenate(
                [
                    jnp.where(here[n], wide(ref[n, pl.ds(first, 1), :]), 0.0),
                    jnp.where(here[n], wide(ref[n, pl.ds(second, 1), :]), 0.0),
                ],
                axis=0,
            )
            for n in range(buckets)
        ]
        total = product(split(jnp.concatenate(values, axis=1)), cell_table[...])
        total = total[:16] + total[16:]
        return total[:8], total[8:]

    cover, salt = per_cell(msg_in, 1, 2)

    for side in range(4):

        @pl.when(inside[sides[side]])
        def _(side=side):
            halo_arrival(side).wait_recv()

        @pl.when(jnp.logical_not(inside[sides[side]]))
        def _(side=side):
            dst = row_in if side < 2 else col_in
            dst[side % 2] = jnp.zeros(dst.shape[1:], F32)

    rows_f = lax.broadcasted_iota(jnp.int32, (fields, 8, width_y), 1)
    top, bottom = rows_f == 0, rows_f == width_x - 1
    leftmost, rightmost = lanes_f == 0, lanes_f == width_y - 1
    sum_x = jnp.zeros((8, width_y), F32)
    sum_y = jnp.zeros((8, width_y), F32)
    for k in range(levels):
        level = ocean[:, k]
        before = jnp.stack([row_in[0, pl.ds(f * levels + k, 1), :] for f in range(fields)])
        after = jnp.stack([row_in[1, pl.ds(f * levels + k, 1), :] for f in range(fields)])
        up = jnp.where(top, before, pltpu.roll(level, 1, 1))
        down = jnp.where(bottom, after, pltpu.roll(level, width_x - 1, 1))
        left_in = pltpu.roll(col_in[0], width_y - k, 2) if k else col_in[0]
        right_in = pltpu.roll(col_in[1], width_y - 1 - k, 2)
        left = jnp.where(leftmost, left_in, pltpu.roll(level, 1, 2))
        right = jnp.where(rightmost, right_in, pltpu.roll(level, width_y - 1, 2))
        above = ocean[:, max(k - 1, 0)]
        below = ocean[:, min(k + 1, levels - 1)]
        centre = 1.0 - 4.0 * DIFFUSE_SIDE - 2.0 * DIFFUSE_DEPTH
        new = (
            centre * level
            + DIFFUSE_SIDE * (up + down + left + right)
            + DIFFUSE_DEPTH * (above + below)
        )
        slope_x, slope_y = down - up, right - left
        sum_x = sum_x + (HALINE_CONTR * slope_x[3] - THERMAL_EXP * slope_x[2])
        sum_y = sum_y + (HALINE_CONTR * slope_y[3] - THERMAL_EXP * slope_y[2])
        ocean_out[0, k] = new[0] + CORIOLIS * level[1] - (0.5 * PRESSURE_COEF) * sum_x
        ocean_out[1, k] = new[1] - CORIOLIS * level[0] - (0.5 * PRESSURE_COEF) * sum_y
        if k == 0:
            ocean_out[2, k] = new[2] + HEAT_COEF * (FREEZE - level[2]) * cover
            ocean_out[3, k] = new[3] + SALT_COEF * salt
        else:
            ocean_out[2, k] = new[2]
            ocean_out[3, k] = new[3]

    for n in others:

        @pl.when(inside[n])
        def _(n=n):
            flux_arrival(n).wait_recv()

        @pl.when(jnp.logical_not(inside[n]))
        def _(n=n):
            flux_in[n] = jnp.zeros((8, slots), F32)

    push_x, push_y = per_cell(flux_in, 0, 4)
    ocean_out[0, 0] += DRAG_COEF * (push_x - ocean[0, 0] * cover)
    ocean_out[1, 0] += DRAG_COEF * (push_y - ocean[1, 0] * cover)

    for n in others:

        @pl.when(inside[n])
        def _(n=n):
            msg_copy(n).wait_send()
            flux_copy(n).wait_send()

    for side in range(4):

        @pl.when(inside[sides[side]])
        def _(side=side):
            halo_copy(side).wait_send()


def shards(mesh_shape, *args):
    args = args[:6] + tuple(a.transpose(1, 0, 2) for a in args[6:])
    ocean_state, floe_state, _, contact_pairs, bond_ends = args[:5]
    couple_cell = args[8]
    fields, levels, width_x, width_y = ocean_state.shape
    tiles, pairs = contact_pairs.shape[1:]
    bond_count = bond_ends.shape[2]
    floes = floe_state.shape[1]
    tile = floes // tiles
    buckets, _, slots = couple_cell.shape
    assert width_x == 8 and 2 * tiles == 8 and tile == slots == width_y == 128
    vmem = pl.BlockSpec(memory_space=pltpu.VMEM)
    dma = pltpu.SemaphoreType.DMA
    return pl.pallas_call(
        functools.partial(kernel, mesh_shape),
        out_shape=(
            jax.ShapeDtypeStruct(ocean_state.shape, F32),
            jax.ShapeDtypeStruct(floe_state.shape, F32),
        ),
        in_specs=[pl.BlockSpec(memory_space=pltpu.HBM)] * 9,
        out_specs=(vmem, vmem),
        scratch_shapes=[
            pltpu.VMEM((buckets, 8, slots), F32),
            pltpu.VMEM((buckets, 8, slots), F32),
            pltpu.VMEM((buckets, 8, slots), F32),
            pltpu.VMEM((buckets, 8, slots), F32),
            pltpu.VMEM((2, fields * levels, width_y), F32),
            pltpu.VMEM((2, fields * levels, width_y), F32),
            pltpu.VMEM((2, fields, width_x, width_y), F32),
            pltpu.VMEM((2, fields, width_x, width_y), F32),
            pltpu.VMEM((floes, pairs + bond_count), BF16),
            pltpu.VMEM((tile, buckets * slots), BF16),
            pltpu.VMEM((width_y, buckets * slots), BF16),
            pltpu.VMEM((2, 2 * tiles, tile), F32),
            pltpu.VMEM((2, 2 * tiles, tile), F32),
            pltpu.VMEM(ocean_state.shape, F32),
            pltpu.VMEM((2, width_x, width_y), F32),
            *[pltpu.VMEM(a.shape, a.dtype) for a in args[1:]],
            dma((10,)),
            dma((buckets,)),
            dma((buckets,)),
            dma((buckets,)),
            dma((buckets,)),
            dma((4,)),
            dma((4,)),
        ],
        compiler_params=pltpu.CompilerParams(
            collective_id=0, has_side_effects=True, vmem_limit_bytes=56 * 1024 * 1024
        ),
        cost_estimate=pl.CostEstimate(
            flops=200_000_000, bytes_accessed=1_000_000, transcendentals=0
        ),
    )(*args)


def solution(mesh):
    in_specs = (
        P(None, None, "ocx", "ocy"),
        P(None, ("ocx", "ocy")),
        P(None, ("ocx", "ocy")),
        P(None, ("ocx", "ocy"), None),
        P(None, ("ocx", "ocy"), None),
        P(("ocx", "ocy"), None),
        P(("ocx", "ocy"), None, None),
        P(("ocx", "ocy"), None, None),
        P(("ocx", "ocy"), None, None),
    )
    out_specs = (P(None, None, "ocx", "ocy"), P(None, ("ocx", "ocy")))
    body = functools.partial(shards, (mesh.shape["ocx"], mesh.shape["ocy"]))
    return jax.shard_map(body, mesh=mesh, in_specs=in_specs, out_specs=out_specs, check_vma=False)
```

```python
import functools

import jax
import jax.numpy as jnp
from jax import lax
from jax.experimental import pallas as pl
from jax.experimental.pallas import tpu as pltpu
from jax.sharding import PartitionSpec as P

SUBSTEPS = 4
TIME_STEP = 0.05
CONTACT_STIFF = 2.0
CONTACT_DAMP = 0.2
BOND_DAMP = 0.3
DRAG_COEF = 0.5
HEAT_COEF = 0.3
SALT_COEF = 0.2
FREEZE = -1.8
DIFFUSE_SIDE = 0.15
DIFFUSE_DEPTH = 0.2
CORIOLIS = 0.3
PRESSURE_COEF = 0.1
THERMAL_EXP = 0.2
HALINE_CONTR = 0.8
MESH = pl.DeviceIdType.MESH
F32 = jnp.float32
BF16 = jnp.bfloat16
CENTRE = 4


def lane_gather(field, index):
    return lax.gather(
        field,
        index[..., None],
        lax.GatherDimensionNumbers(
            offset_dims=(),
            collapsed_slice_dims=(1,),
            start_index_map=(1,),
            operand_batching_dims=(0,),
            start_indices_batching_dims=(0,),
        ),
        slice_sizes=(1, 1),
        mode=lax.GatherScatterMode.PROMISE_IN_BOUNDS,
    )


def split(values):
    high = values.astype(BF16).astype(F32)
    return jnp.concatenate([high, values - high], axis=0).astype(BF16)


def product(values, table):
    return lax.dot_general(
        values, table, (((1,), (1,)), ((), ())), preferred_element_type=F32
    )


def hot(mask):
    return jnp.where(mask, 1.0, 0.0).astype(F32)


def kernel(
    mesh_shape,
    ocean_hbm,
    floe_state_hbm,
    floe_props_hbm,
    contact_hbm,
    bonds_hbm,
    broken_hbm,
    c_floe_hbm,
    c_weight_hbm,
    c_cell_hbm,
    ocean_out,
    floe_out,
    msg,
    msg_in,
    flux,
    flux_in,
    row_out,
    row_in,
    col_out,
    col_in,
    pair_table,
    floe_table,
    cell_table,
    state,
    props,
    ocean,
    surface,
    floe_state,
    floe_props,
    contact,
    bonds,
    broken,
    c_floe,
    c_weight,
    c_cell,
    load_sem,
    msg_send,
    msg_recv,
    flux_send,
    flux_recv,
    halo_send,
    halo_recv,
):
    size_x, size_y = mesh_shape
    fields, levels, width_x, width_y = ocean.shape
    planes = fields * levels
    buckets, slots = c_cell.shape[0], c_cell.shape[2]
    tiles, pairs = contact.shape[1], contact.shape[2]
    bond_count = bonds.shape[2]
    tile = floe_state.shape[1] // tiles
    rows = 2 * tiles
    at_x, at_y = lax.axis_index("ocx"), lax.axis_index("ocy")

    inside = []
    for n in range(buckets):
        dx, dy = n // 3 - 1, n % 3 - 1
        ok_x = {-1: at_x > 0, 0: at_x >= 0, 1: at_x < size_x - 1}[dx]
        ok_y = {-1: at_y > 0, 0: at_y >= 0, 1: at_y < size_y - 1}[dy]
        inside.append(jnp.logical_and(ok_x, ok_y))
    others = [0, 2, 6, 8, 1, 7, 3, 5]
    sides = [1, 7, 3, 5]

    def place(n):
        return (at_x + (n // 3 - 1), at_y + (n % 3 - 1))

    barrier = pltpu.get_barrier_semaphore()
    for n in others:

        @pl.when(inside[n])
        def _(n=n):
            pl.semaphore_signal(barrier, inc=1, device_id=place(n), device_id_type=MESH)

    loads = [
        pltpu.make_async_copy(src, dst, load_sem.at[at])
        for at, (src, dst) in enumerate(
            [
                (c_cell_hbm, c_cell),
                (ocean_hbm.at[pl.ds(0, 2), 0], surface),
                (c_floe_hbm, c_floe),
                (floe_props_hbm, floe_props),
                (c_weight_hbm, c_weight),
                (floe_state_hbm, floe_state),
                (ocean_hbm, ocean),
                (contact_hbm, contact),
                (bonds_hbm, bonds),
                (broken_hbm, broken),
            ]
        )
    ]
    for load in loads:
        load.start()

    def copy(src, dst, send, recv, n):
        return pltpu.make_async_remote_copy(
            src_ref=src,
            dst_ref=dst,
            send_sem=send,
            recv_sem=recv,
            device_id=place(n),
            device_id_type=MESH,
        )

    def msg_copy(n):
        return copy(msg.at[n], msg_in.at[8 - n], msg_send.at[n], msg_recv.at[8 - n], n)

    def flux_copy(n):
        return copy(flux.at[n], flux_in.at[8 - n], flux_send.at[n], flux_recv.at[8 - n], n)

    def halo_copy(side):
        pair = side // 2
        src, dst = (row_out, row_in) if pair == 0 else (col_out, col_in)
        mine, there = side % 2, 1 - side % 2
        return copy(
            src.at[mine],
            dst.at[there],
            halo_send.at[side],
            halo_recv.at[2 * pair + there],
            sides[side],
        )

    def msg_arrival(n):
        return copy(msg.at[8 - n], msg_in.at[n], msg_send.at[8 - n], msg_recv.at[n], n)

    def flux_arrival(n):
        return copy(flux.at[8 - n], flux_in.at[n], flux_send.at[8 - n], flux_recv.at[n], n)

    def halo_arrival(side):
        pair = side // 2
        src, dst = (row_out, row_in) if pair == 0 else (col_out, col_in)
        return copy(
            src.at[1 - side % 2],
            dst.at[side % 2],
            halo_send.at[side],
            halo_recv.at[side],
            sides[side],
        )

    row8 = lax.broadcasted_iota(jnp.int32, (8, width_y), 0)
    lane8 = lax.broadcasted_iota(jnp.int32, (8, width_y), 1)
    low = row8 < tiles
    row_tile = jnp.where(low, row8, row8 - tiles)

    def wide(ref_row):
        return jnp.broadcast_to(ref_row, (8, slots))

    for load in loads[:6]:
        load.wait()

    for t in range(tiles):
        lanes = pl.ds(t * tile, tile)
        for c in range(2):
            state[0, pl.ds(c * tiles + t, 1), :] = floe_state[pl.ds(c, 1), lanes]
            state[1, pl.ds(c * tiles + t, 1), :] = floe_state[pl.ds(2 + c, 1), lanes]
            props[0, pl.ds(c * tiles + t, 1), :] = floe_props[pl.ds(0, 1), lanes]
            props[1, pl.ds(c * tiles + t, 1), :] = floe_props[pl.ds(1, 1), lanes]
    east, north = surface[0], surface[1]
    thick = props[1]
    floe_lane, floe_mask = [], []
    for n in range(buckets):
        cell = wide(c_cell[n])
        cell_row, cell_lane = cell // width_y, cell % width_y
        floe = wide(c_floe[n])
        floe_lane.append(floe % tile)
        floe_mask.append(floe // tile == row_tile)
        weight = wide(c_weight[n])
        here = cell_row == row8
        first = jnp.where(here, lane_gather(east, cell_lane), 0.0)
        second = jnp.where(here, lane_gather(north, cell_lane), 0.0)
        first = first + pltpu.roll(first, 4, 0)
        second = second + pltpu.roll(second, 4, 0)
        both = jnp.where(low, first, second)
        both = both + pltpu.roll(both, 7, 0)
        both = both + pltpu.roll(both, 6, 0)
        msg[n] = both
        other = jnp.where(floe_mask[n], lane_gather(thick, floe_lane[n]), 0.0)
        other = other + pltpu.roll(other, 7, 0)
        other = other + pltpu.roll(other, 6, 0)
        msg[n, pl.ds(1, 1), :] = weight[0:1]
        msg[n, pl.ds(2, 1), :] = weight[0:1] * other[0:1]

    pl.semaphore_wait(barrier, sum(inside[n].astype(jnp.int32) for n in others))
    for n in others:

        @pl.when(inside[n])
        def _(n=n):
            msg_copy(n).start()

    msg_in[CENTRE] = msg[CENTRE]
    for n in others:

        @pl.when(jnp.logical_not(inside[n]))
        def _(n=n):
            msg_in[n] = jnp.zeros((8, slots), F32)
            flux_in[n] = jnp.zeros((8, slots), F32)

    for side in range(4):

        @pl.when(jnp.logical_not(inside[sides[side]]))
        def _(side=side):
            dst = row_in if side < 2 else col_in
            dst[side % 2] = jnp.zeros(dst.shape[1:], F32)

    for load in loads[6:]:
        load.wait()

    flat = ocean.reshape(planes * width_x, width_y)
    row_out[0] = flat[pl.ds(0, planes, stride=width_x), :]
    row_out[1] = flat[pl.ds(width_x - 1, planes, stride=width_x), :]
    lanes_f = lax.broadcasted_iota(jnp.int32, (fields, 8, width_y), 2)
    west = jnp.zeros((fields, 8, width_y), F32)
    side_e = jnp.zeros((fields, 8, width_y), F32)
    for k in range(levels):
        level = ocean[:, k]
        west = jnp.where(lanes_f == k, pltpu.roll(level, k, 2) if k else level, west)
        side_e = jnp.where(lanes_f == k, pltpu.roll(level, k + 1, 2), side_e)
    col_out[0] = west
    col_out[1] = side_e
    for side in range(4):

        @pl.when(inside[sides[side]])
        def _(side=side):
            halo_copy(side).start()

    low_row = lax.broadcasted_iota(jnp.int32, (tile, slots), 0)
    for n in range(buckets):
        floe = c_floe[n] % tile
        cell = c_cell[n] % width_y
        lanes = pl.ds(n * slots, slots)
        floe_table[:, lanes] = hot(low_row == floe).astype(BF16)
        cell_table[:, lanes] = hot(low_row == cell).astype(BF16)
    span = 128
    contact_chunks, bond_chunks = pairs // span, bond_count // span
    wide_row = lax.broadcasted_iota(jnp.int32, (tile, span), 0)
    for t in range(tiles):
        for c in range(contact_chunks + bond_chunks):
            ref, at = (contact, c) if c < contact_chunks else (bonds, c - contact_chunks)
            lanes = pl.ds(at * span, span)
            head = ref[0, pl.ds(t, 1), lanes]
            tail = ref[1, pl.ds(t, 1), lanes]
            pair_table[pl.ds(c * span, span), pl.ds(t * tile, tile)] = (
                (hot(wide_row == head) - hot(wide_row == tail)).T.astype(BF16)
            )

    def twice(array):
        return jnp.concatenate([array, array], axis=0)

    positions, velocity = state[0], state[1]
    radius = props[0]
    inv_mass = TIME_STEP / (thick * radius * radius)
    ends, inv_reach = [], []
    for c in range(contact_chunks):
        lanes = pl.ds(c * span, span)
        head, tail = twice(contact[0, :, lanes]), twice(contact[1, :, lanes])
        reach = lane_gather(radius, head) + lane_gather(radius, tail)
        ends.append((head, tail))
        inv_reach.append(1.0 / (reach * reach))
    bond_ends, bond_coef = [], []
    for c in range(bond_chunks):
        lanes = pl.ds(c * span, span)
        bond_ends.append((twice(bonds[0, :, lanes]), twice(bonds[1, :, lanes])))
        bond_coef.append(BOND_DAMP * (1 - twice(broken[:, lanes])).astype(F32))

    def contact_force(positions, velocity):
        forces = []
        for (head, tail), inv in zip(ends, inv_reach):
            separation = lane_gather(positions, tail) - lane_gather(positions, head)
            relative = lane_gather(velocity, tail) - lane_gather(velocity, head)
            square = separation * separation
            square = square + pltpu.roll(square, tiles, 0)
            depth = jnp.maximum(1.0 - square * inv, 0.0)
            forces.append(depth * (CONTACT_DAMP * relative - CONTACT_STIFF * separation))
        for (head, tail), coef in zip(bond_ends, bond_coef):
            forces.append(coef * (lane_gather(velocity, tail) - lane_gather(velocity, head)))
        spread = jnp.dot(split(jnp.concatenate(forces, axis=1)), pair_table[...], preferred_element_type=F32)
        spread = spread[:rows] + spread[rows:]
        total = jnp.zeros((rows, tile), F32)
        for t in range(tiles):
            total = jnp.where(row_tile == t, spread[:, t * tile : (t + 1) * tile], total)
        return total

    force = contact_force(positions, velocity)

    def per_floe(values):
        total = product(split(jnp.concatenate(values, axis=1)), floe_table[...])
        return total[:rows] + total[rows:]

    weights = [wide(c_weight[n]) for n in range(buckets)]
    masked = [jnp.where(m, w, 0.0) for m, w in zip(floe_mask, weights)]
    area = DRAG_COEF * per_floe(masked)

    for n in others:

        @pl.when(inside[n])
        def _(n=n):
            msg_arrival(n).wait_recv()

    samples = [
        jnp.where(low, wide(msg_in[n, pl.ds(0, 1), :]), wide(msg_in[n, pl.ds(4, 1), :]))
        for n in range(buckets)
    ]
    drag = DRAG_COEF * per_floe([m * s for m, s in zip(masked, samples)])

    mean_vel = jnp.zeros_like(velocity)
    for substep in range(SUBSTEPS):
        if substep:
            force = contact_force(positions, velocity)
        velocity = velocity + inv_mass * (drag - area * velocity + force)
        positions = positions + TIME_STEP * velocity
        mean_vel = mean_vel + velocity / SUBSTEPS

    for n in range(buckets):
        speed = jnp.where(floe_mask[n], lane_gather(mean_vel, floe_lane[n]), 0.0)
        speed = speed + pltpu.roll(speed, 7, 0)
        speed = speed + pltpu.roll(speed, 6, 0)
        flux[n] = weights[n] * speed
    for n in others:

        @pl.when(inside[n])
        def _(n=n):
            flux_copy(n).start()

    flux_in[CENTRE] = flux[CENTRE]
    state[0] = positions
    state[1] = velocity
    for t in range(tiles):
        lanes = pl.ds(t * tile, tile)
        for c in range(2):
            floe_out[pl.ds(c, 1), lanes] = state[0, pl.ds(c * tiles + t, 1), :]
            floe_out[pl.ds(2 + c, 1), lanes] = state[1, pl.ds(c * tiles + t, 1), :]

    here = [
        c_cell[n] // width_y == row8 for n in range(buckets)
    ]

    def per_cell(ref, first, second):
        values = [
            jnp.concatenate(
                [
                    jnp.where(here[n], wide(ref[n, pl.ds(first, 1), :]), 0.0),
                    jnp.where(here[n], wide(ref[n, pl.ds(second, 1), :]), 0.0),
                ],
                axis=0,
            )
            for n in range(buckets)
        ]
        total = product(split(jnp.concatenate(values, axis=1)), cell_table[...])
        total = total[:16] + total[16:]
        return total[:8], total[8:]

    cover, salt = per_cell(msg_in, 1, 2)

    for side in range(4):

        @pl.when(inside[sides[side]])
        def _(side=side):
            halo_arrival(side).wait_recv()

    rows_f = lax.broadcasted_iota(jnp.int32, (fields, 8, width_y), 1)
    top, bottom = rows_f == 0, rows_f == width_x - 1
    leftmost, rightmost = lanes_f == 0, lanes_f == width_y - 1
    sum_x = jnp.zeros((8, width_y), F32)
    sum_y = jnp.zeros((8, width_y), F32)
    for k in range(levels):
        level = ocean[:, k]
        before = jnp.stack([row_in[0, pl.ds(f * levels + k, 1), :] for f in range(fields)])
        after = jnp.stack([row_in[1, pl.ds(f * levels + k, 1), :] for f in range(fields)])
        up = jnp.where(top, before, pltpu.roll(level, 1, 1))
        down = jnp.where(bottom, after, pltpu.roll(level, width_x - 1, 1))
        left_in = pltpu.roll(col_in[0], width_y - k, 2) if k else col_in[0]
        right_in = pltpu.roll(col_in[1], width_y - 1 - k, 2)
        left = jnp.where(leftmost, left_in, pltpu.roll(level, 1, 2))
        right = jnp.where(rightmost, right_in, pltpu.roll(level, width_y - 1, 2))
        above = ocean[:, max(k - 1, 0)]
        below = ocean[:, min(k + 1, levels - 1)]
        centre = 1.0 - 4.0 * DIFFUSE_SIDE - 2.0 * DIFFUSE_DEPTH
        new = (
            centre * level
            + DIFFUSE_SIDE * (up + down + left + right)
            + DIFFUSE_DEPTH * (above + below)
        )
        slope_x, slope_y = down - up, right - left
        sum_x = sum_x + (HALINE_CONTR * slope_x[3] - THERMAL_EXP * slope_x[2])
        sum_y = sum_y + (HALINE_CONTR * slope_y[3] - THERMAL_EXP * slope_y[2])
        ocean_out[0, k] = new[0] + CORIOLIS * level[1] - (0.5 * PRESSURE_COEF) * sum_x
        ocean_out[1, k] = new[1] - CORIOLIS * level[0] - (0.5 * PRESSURE_COEF) * sum_y
        if k == 0:
            ocean_out[2, k] = new[2] + HEAT_COEF * (FREEZE - level[2]) * cover
            ocean_out[3, k] = new[3] + SALT_COEF * salt
        else:
            ocean_out[2, k] = new[2]
            ocean_out[3, k] = new[3]

    for n in others:

        @pl.when(inside[n])
        def _(n=n):
            flux_arrival(n).wait_recv()

    push_x, push_y = per_cell(flux_in, 0, 4)
    ocean_out[0, 0] += DRAG_COEF * (push_x - ocean[0, 0] * cover)
    ocean_out[1, 0] += DRAG_COEF * (push_y - ocean[1, 0] * cover)

    for n in others:

        @pl.when(inside[n])
        def _(n=n):
            msg_copy(n).wait_send()
            flux_copy(n).wait_send()

    for side in range(4):

        @pl.when(inside[sides[side]])
        def _(side=side):
            halo_copy(side).wait_send()


def store(ocean, floes, ocean_out, floe_out, sem):
    first = pltpu.make_async_copy(ocean, ocean_out, sem.at[0])
    second = pltpu.make_async_copy(floes, floe_out, sem.at[1])
    first.start()
    second.start()
    first.wait()
    second.wait()


def shards(mesh_shape, *args):
    args = args[:6] + tuple(a.transpose(1, 0, 2) for a in args[6:])
    ocean_state, floe_state, _, contact_pairs, bond_ends = args[:5]
    couple_cell = args[8]
    fields, levels, width_x, width_y = ocean_state.shape
    tiles, pairs = contact_pairs.shape[1:]
    bond_count = bond_ends.shape[2]
    floes = floe_state.shape[1]
    tile = floes // tiles
    buckets, _, slots = couple_cell.shape
    assert width_x == 8 and 2 * tiles == 8 and tile == slots == width_y == 128
    vmem = pl.BlockSpec(memory_space=pltpu.VMEM)
    dma = pltpu.SemaphoreType.DMA
    results = pl.pallas_call(
        functools.partial(kernel, mesh_shape),
        out_shape=(
            pltpu.VMEM(ocean_state.shape, F32),
            pltpu.VMEM(floe_state.shape, F32),
        ),
        in_specs=[pl.BlockSpec(memory_space=pltpu.HBM)] * 9,
        out_specs=(vmem, vmem),
        scratch_shapes=[
            pltpu.VMEM((buckets, 8, slots), F32),
            pltpu.VMEM((buckets, 8, slots), F32),
            pltpu.VMEM((buckets, 8, slots), F32),
            pltpu.VMEM((buckets, 8, slots), F32),
            pltpu.VMEM((2, fields * levels, width_y), F32),
            pltpu.VMEM((2, fields * levels, width_y), F32),
            pltpu.VMEM((2, fields, width_x, width_y), F32),
            pltpu.VMEM((2, fields, width_x, width_y), F32),
            pltpu.VMEM((pairs + bond_count, floes), BF16),
            pltpu.VMEM((tile, buckets * slots), BF16),
            pltpu.VMEM((width_y, buckets * slots), BF16),
            pltpu.VMEM((2, 2 * tiles, tile), F32),
            pltpu.VMEM((2, 2 * tiles, tile), F32),
            pltpu.VMEM(ocean_state.shape, F32),
            pltpu.VMEM((2, width_x, width_y), F32),
            *[pltpu.VMEM(a.shape, a.dtype) for a in args[1:]],
            dma((10,)),
            dma((buckets,)),
            dma((buckets,)),
            dma((buckets,)),
            dma((buckets,)),
            dma((4,)),
            dma((4,)),
        ],
        compiler_params=pltpu.CompilerParams(
            collective_id=0, has_side_effects=True, vmem_limit_bytes=56 * 1024 * 1024
        ),
        cost_estimate=pl.CostEstimate(
            flops=200_000_000, bytes_accessed=1_000_000, transcendentals=0
        ),
    )(*args)
    results = [pltpu.with_memory_space_constraint(r, pltpu.VMEM) for r in results]
    hbm = pl.BlockSpec(memory_space=pltpu.HBM)
    return pl.pallas_call(
        store,
        out_shape=(
            jax.ShapeDtypeStruct(ocean_state.shape, F32),
            jax.ShapeDtypeStruct(floe_state.shape, F32),
        ),
        in_specs=[vmem] * 2,
        out_specs=(hbm, hbm),
        scratch_shapes=[dma((2,))],
    )(*results)


def solution(mesh):
    in_specs = (
        P(None, None, "ocx", "ocy"),
        P(None, ("ocx", "ocy")),
        P(None, ("ocx", "ocy")),
        P(None, ("ocx", "ocy"), None),
        P(None, ("ocx", "ocy"), None),
        P(("ocx", "ocy"), None),
        P(("ocx", "ocy"), None, None),
        P(("ocx", "ocy"), None, None),
        P(("ocx", "ocy"), None, None),
    )
    out_specs = (P(None, None, "ocx", "ocy"), P(None, ("ocx", "ocy")))
    body = functools.partial(shards, (mesh.shape["ocx"], mesh.shape["ocy"]))
    return jax.shard_map(body, mesh=mesh, in_specs=in_specs, out_specs=out_specs, check_vma=False)
```

```python
import functools

import jax
import jax.numpy as jnp
from jax import lax
from jax.experimental import pallas as pl
from jax.experimental.pallas import tpu as pltpu
from jax.sharding import PartitionSpec as P

SUBSTEPS = 4
TIME_STEP = 0.05
CONTACT_STIFF = 2.0
CONTACT_DAMP = 0.2
BOND_DAMP = 0.3
DRAG_COEF = 0.5
HEAT_COEF = 0.3
SALT_COEF = 0.2
FREEZE = -1.8
DIFFUSE_SIDE = 0.15
DIFFUSE_DEPTH = 0.2
CORIOLIS = 0.3
PRESSURE_COEF = 0.1
THERMAL_EXP = 0.2
HALINE_CONTR = 0.8
MESH = pl.DeviceIdType.MESH
F32 = jnp.float32
BF16 = jnp.bfloat16
CENTRE = 4


def lane_gather(field, index):
    return lax.gather(
        field,
        index[..., None],
        lax.GatherDimensionNumbers(
            offset_dims=(),
            collapsed_slice_dims=(1,),
            start_index_map=(1,),
            operand_batching_dims=(0,),
            start_indices_batching_dims=(0,),
        ),
        slice_sizes=(1, 1),
        mode=lax.GatherScatterMode.PROMISE_IN_BOUNDS,
    )


def split(values):
    high = values.astype(BF16).astype(F32)
    return jnp.concatenate([high, values - high], axis=0).astype(BF16)


def product(values, table):
    return lax.dot_general(
        values, table, (((1,), (0,)), ((), ())), preferred_element_type=F32
    )


def hot(mask):
    return jnp.where(mask, 1.0, 0.0).astype(F32)


def kernel(
    mesh_shape,
    ocean_hbm,
    floe_state_hbm,
    floe_props_hbm,
    contact_hbm,
    bonds_hbm,
    broken_hbm,
    c_floe_hbm,
    c_weight_hbm,
    c_cell_hbm,
    ocean_out,
    floe_out,
    msg,
    msg_in,
    flux,
    flux_in,
    row_out,
    row_in,
    col_out,
    col_in,
    pair_table,
    floe_table,
    cell_table,
    state,
    props,
    ocean,
    surface,
    floe_state,
    floe_props,
    contact,
    bonds,
    broken,
    c_floe,
    c_weight,
    c_cell,
    load_sem,
    msg_send,
    msg_recv,
    flux_send,
    flux_recv,
    halo_send,
    halo_recv,
):
    size_x, size_y = mesh_shape
    fields, levels, width_x, width_y = ocean.shape
    planes = fields * levels
    buckets, slots = c_cell.shape[0], c_cell.shape[2]
    tiles, pairs = contact.shape[1], contact.shape[2]
    bond_count = bonds.shape[2]
    tile = floe_state.shape[1] // tiles
    rows = 2 * tiles
    at_x, at_y = lax.axis_index("ocx"), lax.axis_index("ocy")

    inside = []
    for n in range(buckets):
        dx, dy = n // 3 - 1, n % 3 - 1
        ok_x = {-1: at_x > 0, 0: at_x >= 0, 1: at_x < size_x - 1}[dx]
        ok_y = {-1: at_y > 0, 0: at_y >= 0, 1: at_y < size_y - 1}[dy]
        inside.append(jnp.logical_and(ok_x, ok_y))
    others = [0, 2, 6, 8, 1, 7, 3, 5]
    sides = [1, 7, 3, 5]

    def place(n):
        return (at_x + (n // 3 - 1), at_y + (n % 3 - 1))

    barrier = pltpu.get_barrier_semaphore()
    for n in others:

        @pl.when(inside[n])
        def _(n=n):
            pl.semaphore_signal(barrier, inc=1, device_id=place(n), device_id_type=MESH)

    loads = [
        pltpu.make_async_copy(src, dst, load_sem.at[at])
        for at, (src, dst) in enumerate(
            [
                (c_cell_hbm, c_cell),
                (ocean_hbm.at[pl.ds(0, 2), 0], surface),
                (c_floe_hbm, c_floe),
                (floe_props_hbm, floe_props),
                (c_weight_hbm, c_weight),
                (floe_state_hbm, floe_state),
                (ocean_hbm, ocean),
                (contact_hbm, contact),
                (bonds_hbm, bonds),
                (broken_hbm, broken),
            ]
        )
    ]
    for load in loads:
        load.start()

    def copy(src, dst, send, recv, n):
        return pltpu.make_async_remote_copy(
            src_ref=src,
            dst_ref=dst,
            send_sem=send,
            recv_sem=recv,
            device_id=place(n),
            device_id_type=MESH,
        )

    def msg_copy(n):
        return copy(msg.at[n], msg_in.at[8 - n], msg_send.at[n], msg_recv.at[8 - n], n)

    def flux_copy(n):
        return copy(flux.at[n], flux_in.at[8 - n], flux_send.at[n], flux_recv.at[8 - n], n)

    def halo_copy(side):
        pair = side // 2
        src, dst = (row_out, row_in) if pair == 0 else (col_out, col_in)
        mine, there = side % 2, 1 - side % 2
        return copy(
            src.at[mine],
            dst.at[there],
            halo_send.at[side],
            halo_recv.at[2 * pair + there],
            sides[side],
        )

    def msg_arrival(n):
        return copy(msg.at[8 - n], msg_in.at[n], msg_send.at[8 - n], msg_recv.at[n], n)

    def flux_arrival(n):
        return copy(flux.at[8 - n], flux_in.at[n], flux_send.at[8 - n], flux_recv.at[n], n)

    def halo_arrival(side):
        pair = side // 2
        src, dst = (row_out, row_in) if pair == 0 else (col_out, col_in)
        return copy(
            src.at[1 - side % 2],
            dst.at[side % 2],
            halo_send.at[side],
            halo_recv.at[side],
            sides[side],
        )

    row8 = lax.broadcasted_iota(jnp.int32, (8, width_y), 0)
    lane8 = lax.broadcasted_iota(jnp.int32, (8, width_y), 1)
    low = row8 < tiles
    row_tile = jnp.where(low, row8, row8 - tiles)

    def wide(ref_row):
        return jnp.broadcast_to(ref_row, (8, slots))

    for load in loads[:6]:
        load.wait()

    for t in range(tiles):
        lanes = pl.ds(t * tile, tile)
        for c in range(2):
            state[0, pl.ds(c * tiles + t, 1), :] = floe_state[pl.ds(c, 1), lanes]
            state[1, pl.ds(c * tiles + t, 1), :] = floe_state[pl.ds(2 + c, 1), lanes]
            props[0, pl.ds(c * tiles + t, 1), :] = floe_props[pl.ds(0, 1), lanes]
            props[1, pl.ds(c * tiles + t, 1), :] = floe_props[pl.ds(1, 1), lanes]
    east, north = surface[0], surface[1]
    thick = props[1]
    floe_lane, floe_mask = [], []
    for n in range(buckets):
        cell = wide(c_cell[n])
        cell_row, cell_lane = cell // width_y, cell % width_y
        floe = wide(c_floe[n])
        floe_lane.append(floe % tile)
        floe_mask.append(floe // tile == row_tile)
        weight = wide(c_weight[n])
        here = cell_row == row8
        first = jnp.where(here, lane_gather(east, cell_lane), 0.0)
        second = jnp.where(here, lane_gather(north, cell_lane), 0.0)
        first = first + pltpu.roll(first, 4, 0)
        second = second + pltpu.roll(second, 4, 0)
        both = jnp.where(low, first, second)
        both = both + pltpu.roll(both, 7, 0)
        both = both + pltpu.roll(both, 6, 0)
        msg[n] = both
        other = jnp.where(floe_mask[n], lane_gather(thick, floe_lane[n]), 0.0)
        other = other + pltpu.roll(other, 7, 0)
        other = other + pltpu.roll(other, 6, 0)
        msg[n, pl.ds(1, 1), :] = weight[0:1]
        msg[n, pl.ds(2, 1), :] = weight[0:1] * other[0:1]

    pl.semaphore_wait(barrier, sum(inside[n].astype(jnp.int32) for n in others))
    for n in others:

        @pl.when(inside[n])
        def _(n=n):
            msg_copy(n).start()

    msg_in[CENTRE] = msg[CENTRE]
    for n in others:

        @pl.when(jnp.logical_not(inside[n]))
        def _(n=n):
            msg_in[n] = jnp.zeros((8, slots), F32)
            flux_in[n] = jnp.zeros((8, slots), F32)

    for side in range(4):

        @pl.when(jnp.logical_not(inside[sides[side]]))
        def _(side=side):
            dst = row_in if side < 2 else col_in
            dst[side % 2] = jnp.zeros(dst.shape[1:], F32)

    for load in loads[6:]:
        load.wait()

    flat = ocean.reshape(planes * width_x, width_y)
    row_out[0] = flat[pl.ds(0, planes, stride=width_x), :]
    row_out[1] = flat[pl.ds(width_x - 1, planes, stride=width_x), :]
    lanes_f = lax.broadcasted_iota(jnp.int32, (fields, 8, width_y), 2)
    west = jnp.zeros((fields, 8, width_y), F32)
    side_e = jnp.zeros((fields, 8, width_y), F32)
    for k in range(levels):
        level = ocean[:, k]
        west = jnp.where(lanes_f == k, pltpu.roll(level, k, 2) if k else level, west)
        side_e = jnp.where(lanes_f == k, pltpu.roll(level, k + 1, 2), side_e)
    col_out[0] = west
    col_out[1] = side_e
    for side in range(4):

        @pl.when(inside[sides[side]])
        def _(side=side):
            halo_copy(side).start()

    low_row = lax.broadcasted_iota(jnp.int32, (tile, slots), 0)
    for n in range(buckets):
        floe = c_floe[n] % tile
        lanes = pl.ds(n * slots, slots)
        floe_table[lanes, :] = hot(low_row == floe).T.astype(BF16)
    span = 128
    contact_chunks, bond_chunks = pairs // span, bond_count // span
    wide_row = lax.broadcasted_iota(jnp.int32, (tile, span), 0)
    for t in range(tiles):
        for c in range(contact_chunks + bond_chunks):
            ref, at = (contact, c) if c < contact_chunks else (bonds, c - contact_chunks)
            lanes = pl.ds(at * span, span)
            head = ref[0, pl.ds(t, 1), lanes]
            tail = ref[1, pl.ds(t, 1), lanes]
            pair_table[pl.ds(c * span, span), pl.ds(t * tile, tile)] = (
                (hot(wide_row == head) - hot(wide_row == tail)).T.astype(BF16)
            )

    def twice(array):
        return jnp.concatenate([array, array], axis=0)

    positions, velocity = state[0], state[1]
    radius = props[0]
    inv_mass = TIME_STEP / (thick * radius * radius)
    ends, inv_reach = [], []
    for c in range(contact_chunks):
        lanes = pl.ds(c * span, span)
        head, tail = twice(contact[0, :, lanes]), twice(contact[1, :, lanes])
        reach = lane_gather(radius, head) + lane_gather(radius, tail)
        ends.append((head, tail))
        inv_reach.append(1.0 / (reach * reach))
    bond_ends, bond_coef = [], []
    for c in range(bond_chunks):
        lanes = pl.ds(c * span, span)
        bond_ends.append((twice(bonds[0, :, lanes]), twice(bonds[1, :, lanes])))
        bond_coef.append(BOND_DAMP * (1 - twice(broken[:, lanes])).astype(F32))

    def contact_force(positions, velocity):
        forces = []
        for (head, tail), inv in zip(ends, inv_reach):
            separation = lane_gather(positions, tail) - lane_gather(positions, head)
            relative = lane_gather(velocity, tail) - lane_gather(velocity, head)
            square = separation * separation
            square = square + pltpu.roll(square, tiles, 0)
            depth = jnp.maximum(1.0 - square * inv, 0.0)
            forces.append(depth * (CONTACT_DAMP * relative - CONTACT_STIFF * separation))
        for (head, tail), coef in zip(bond_ends, bond_coef):
            forces.append(coef * (lane_gather(velocity, tail) - lane_gather(velocity, head)))
        spread = jnp.dot(split(jnp.concatenate(forces, axis=1)), pair_table[...], preferred_element_type=F32)
        spread = spread[:rows] + spread[rows:]
        total = jnp.zeros((rows, tile), F32)
        for t in range(tiles):
            total = jnp.where(row_tile == t, spread[:, t * tile : (t + 1) * tile], total)
        return total

    force = contact_force(positions, velocity)

    def per_floe(values):
        total = product(split(jnp.concatenate(values, axis=1)), floe_table[...])
        return total[:rows] + total[rows:]

    weights = [wide(c_weight[n]) for n in range(buckets)]
    masked = [jnp.where(m, w, 0.0) for m, w in zip(floe_mask, weights)]
    area = DRAG_COEF * per_floe(masked)

    for n in others:

        @pl.when(inside[n])
        def _(n=n):
            msg_arrival(n).wait_recv()

    samples = [
        jnp.where(low, wide(msg_in[n, pl.ds(0, 1), :]), wide(msg_in[n, pl.ds(4, 1), :]))
        for n in range(buckets)
    ]
    drag = DRAG_COEF * per_floe([m * s for m, s in zip(masked, samples)])

    mean_vel = jnp.zeros_like(velocity)
    for substep in range(SUBSTEPS):
        if substep:
            force = contact_force(positions, velocity)
        velocity = velocity + inv_mass * (drag - area * velocity + force)
        positions = positions + TIME_STEP * velocity
        mean_vel = mean_vel + velocity / SUBSTEPS

    for n in range(buckets):
        speed = jnp.where(floe_mask[n], lane_gather(mean_vel, floe_lane[n]), 0.0)
        speed = speed + pltpu.roll(speed, 7, 0)
        speed = speed + pltpu.roll(speed, 6, 0)
        flux[n] = weights[n] * speed
    for n in others:

        @pl.when(inside[n])
        def _(n=n):
            flux_copy(n).start()

    flux_in[CENTRE] = flux[CENTRE]
    state[0] = positions
    state[1] = velocity
    for t in range(tiles):
        lanes = pl.ds(t * tile, tile)
        for c in range(2):
            floe_out[pl.ds(c, 1), lanes] = state[0, pl.ds(c * tiles + t, 1), :]
            floe_out[pl.ds(2 + c, 1), lanes] = state[1, pl.ds(c * tiles + t, 1), :]

    here = [
        c_cell[n] // width_y == row8 for n in range(buckets)
    ]

    def per_cell(ref, first, second):
        values = [
            jnp.concatenate(
                [
                    jnp.where(here[n], wide(ref[n, pl.ds(first, 1), :]), 0.0),
                    jnp.where(here[n], wide(ref[n, pl.ds(second, 1), :]), 0.0),
                ],
                axis=0,
            )
            for n in range(buckets)
        ]
        total = product(split(jnp.concatenate(values, axis=1)), cell_table[...])
        total = total[:16] + total[16:]
        return total[:8], total[8:]

    for n in range(buckets):
        cells = hot(low_row == c_cell[n] % width_y)
        cell_table[pl.ds(n * slots, slots), :] = cells.T.astype(BF16)
    cover, salt = per_cell(msg_in, 1, 2)

    for side in range(4):

        @pl.when(inside[sides[side]])
        def _(side=side):
            halo_arrival(side).wait_recv()

    rows_f = lax.broadcasted_iota(jnp.int32, (fields, 8, width_y), 1)
    top, bottom = rows_f == 0, rows_f == width_x - 1
    leftmost, rightmost = lanes_f == 0, lanes_f == width_y - 1
    sum_x = jnp.zeros((8, width_y), F32)
    sum_y = jnp.zeros((8, width_y), F32)
    for k in range(levels):
        level = ocean[:, k]
        before = jnp.stack([row_in[0, pl.ds(f * levels + k, 1), :] for f in range(fields)])
        after = jnp.stack([row_in[1, pl.ds(f * levels + k, 1), :] for f in range(fields)])
        up = jnp.where(top, before, pltpu.roll(level, 1, 1))
        down = jnp.where(bottom, after, pltpu.roll(level, width_x - 1, 1))
        left_in = pltpu.roll(col_in[0], width_y - k, 2) if k else col_in[0]
        right_in = pltpu.roll(col_in[1], width_y - 1 - k, 2)
        left = jnp.where(leftmost, left_in, pltpu.roll(level, 1, 2))
        right = jnp.where(rightmost, right_in, pltpu.roll(level, width_y - 1, 2))
        above = ocean[:, max(k - 1, 0)]
        below = ocean[:, min(k + 1, levels - 1)]
        centre = 1.0 - 4.0 * DIFFUSE_SIDE - 2.0 * DIFFUSE_DEPTH
        new = (
            centre * level
            + DIFFUSE_SIDE * (up + down + left + right)
            + DIFFUSE_DEPTH * (above + below)
        )
        slope_x, slope_y = down - up, right - left
        sum_x = sum_x + (HALINE_CONTR * slope_x[3] - THERMAL_EXP * slope_x[2])
        sum_y = sum_y + (HALINE_CONTR * slope_y[3] - THERMAL_EXP * slope_y[2])
        ocean_out[0, k] = new[0] + CORIOLIS * level[1] - (0.5 * PRESSURE_COEF) * sum_x
        ocean_out[1, k] = new[1] - CORIOLIS * level[0] - (0.5 * PRESSURE_COEF) * sum_y
        if k == 0:
            ocean_out[2, k] = new[2] + HEAT_COEF * (FREEZE - level[2]) * cover
            ocean_out[3, k] = new[3] + SALT_COEF * salt
        else:
            ocean_out[2, k] = new[2]
            ocean_out[3, k] = new[3]

    for n in others:

        @pl.when(inside[n])
        def _(n=n):
            flux_arrival(n).wait_recv()

    push_x, push_y = per_cell(flux_in, 0, 4)
    ocean_out[0, 0] += DRAG_COEF * (push_x - ocean[0, 0] * cover)
    ocean_out[1, 0] += DRAG_COEF * (push_y - ocean[1, 0] * cover)

    for n in others:

        @pl.when(inside[n])
        def _(n=n):
            msg_copy(n).wait_send()
            flux_copy(n).wait_send()

    for side in range(4):

        @pl.when(inside[sides[side]])
        def _(side=side):
            halo_copy(side).wait_send()


def store(ocean, floes, ocean_out, floe_out, sem):
    first = pltpu.make_async_copy(ocean, ocean_out, sem.at[0])
    second = pltpu.make_async_copy(floes, floe_out, sem.at[1])
    first.start()
    second.start()
    first.wait()
    second.wait()


def shards(mesh_shape, *args):
    args = args[:6] + tuple(a.transpose(1, 0, 2) for a in args[6:])
    ocean_state, floe_state, _, contact_pairs, bond_ends = args[:5]
    couple_cell = args[8]
    fields, levels, width_x, width_y = ocean_state.shape
    tiles, pairs = contact_pairs.shape[1:]
    bond_count = bond_ends.shape[2]
    floes = floe_state.shape[1]
    tile = floes // tiles
    buckets, _, slots = couple_cell.shape
    assert width_x == 8 and 2 * tiles == 8 and tile == slots == width_y == 128
    vmem = pl.BlockSpec(memory_space=pltpu.VMEM)
    dma = pltpu.SemaphoreType.DMA
    results = pl.pallas_call(
        functools.partial(kernel, mesh_shape),
        out_shape=(
            pltpu.VMEM(ocean_state.shape, F32),
            pltpu.VMEM(floe_state.shape, F32),
        ),
        in_specs=[pl.BlockSpec(memory_space=pltpu.HBM)] * 9,
        out_specs=(vmem, vmem),
        scratch_shapes=[
            pltpu.VMEM((buckets, 8, slots), F32),
            pltpu.VMEM((buckets, 8, slots), F32),
            pltpu.VMEM((buckets, 8, slots), F32),
            pltpu.VMEM((buckets, 8, slots), F32),
            pltpu.VMEM((2, fields * levels, width_y), F32),
            pltpu.VMEM((2, fields * levels, width_y), F32),
            pltpu.VMEM((2, fields, width_x, width_y), F32),
            pltpu.VMEM((2, fields, width_x, width_y), F32),
            pltpu.VMEM((pairs + bond_count, floes), BF16),
            pltpu.VMEM((buckets * slots, tile), BF16),
            pltpu.VMEM((buckets * slots, width_y), BF16),
            pltpu.VMEM((2, 2 * tiles, tile), F32),
            pltpu.VMEM((2, 2 * tiles, tile), F32),
            pltpu.VMEM(ocean_state.shape, F32),
            pltpu.VMEM((2, width_x, width_y), F32),
            *[pltpu.VMEM(a.shape, a.dtype) for a in args[1:]],
            dma((10,)),
            dma((buckets,)),
            dma((buckets,)),
            dma((buckets,)),
            dma((buckets,)),
            dma((4,)),
            dma((4,)),
        ],
        compiler_params=pltpu.CompilerParams(
            collective_id=0, has_side_effects=True, vmem_limit_bytes=56 * 1024 * 1024
        ),
        cost_estimate=pl.CostEstimate(
            flops=200_000_000, bytes_accessed=1_000_000, transcendentals=0
        ),
    )(*args)
    results = [pltpu.with_memory_space_constraint(r, pltpu.VMEM) for r in results]
    hbm = pl.BlockSpec(memory_space=pltpu.HBM)
    return pl.pallas_call(
        store,
        out_shape=(
            jax.ShapeDtypeStruct(ocean_state.shape, F32),
            jax.ShapeDtypeStruct(floe_state.shape, F32),
        ),
        in_specs=[vmem] * 2,
        out_specs=(hbm, hbm),
        scratch_shapes=[dma((2,))],
    )(*results)


def solution(mesh):
    in_specs = (
        P(None, None, "ocx", "ocy"),
        P(None, ("ocx", "ocy")),
        P(None, ("ocx", "ocy")),
        P(None, ("ocx", "ocy"), None),
        P(None, ("ocx", "ocy"), None),
        P(("ocx", "ocy"), None),
        P(("ocx", "ocy"), None, None),
        P(("ocx", "ocy"), None, None),
        P(("ocx", "ocy"), None, None),
    )
    out_specs = (P(None, None, "ocx", "ocy"), P(None, ("ocx", "ocy")))
    body = functools.partial(shards, (mesh.shape["ocx"], mesh.shape["ocy"]))
    return jax.shard_map(body, mesh=mesh, in_specs=in_specs, out_specs=out_specs, check_vma=False)
```
